32 devices in a mesh: dp: 8 (over z, y), sub: 4 (over x, core).
Axes of the slice: x: 2, y: 2, z: 4, core: 2. Of those that a mesh axis runs over, the one named last changes fastest.
Arguments:
- inputs: bfloat16 [1024, 32, 2048], P('sub', 'dp'), may hold values from -6 to 6
- w_master: float32 [2048, 6144], replicated, may hold values from -0.125 to 0.125
- v_forget: float32 [2048], replicated, may hold values from -1 to 1
- v_reset: float32 [2048], replicated, may hold values from -1 to 1
- b_forget: float32 [2048], replicated, may hold values from -1 to 9
- b_reset: float32 [2048], replicated, may hold values from -2 to 2
- ln_gain: float32 [2048], replicated, may hold values from 0.5 to 1.5
- ln_shift: float32 [2048], replicated, may hold values from -0.5 to 0.5
- resets: int32 [1024, 32], P('sub', 'dp'), may hold values from 0 to 1, as said below
- cotangent: bfloat16 [1024, 32, 2048], P('sub', 'dp'), may hold values from -6 to 6
Outputs:
- output: bfloat16 [1024, 32, 2048], P('sub', 'dp')
- input_grad: float32 [1024, 32, 2048], P('sub', 'dp')
- w_grad: float32 [2048, 6144], replicated
- v_forget_grad: float32 [2048], replicated
- v_reset_grad: float32 [2048], replicated
- b_forget_grad: float32 [2048], replicated
- b_reset_grad: float32 [2048], replicated
- gain_grad: float32 [2048], replicated
- shift_grad: float32 [2048], replicated
- final_state: float32 [32, 2048], P('dp', 'sub')
The draws below stay inside these ranges and needn't reach their ends.
Inputs may be any that keep to these rules, and one draw needn't show every extreme that they name: `resets`: in each block of 4 sequences that share an index of dp, one sequence has no reset at all and some other has one at position 512.
All inputs are finite; a program needn't handle non-finite values.
Results may differ from the reference program's by a relative error of at most 0.0079.
Values sent between devices are 32-bit elements; how exact they have to be, the bound alone decides.
A program may use at most 384 MiB of HBM per device.

```python
import jax
import jax.numpy as jnp
from jax import lax

D = 2048
LENGTH = 1024
SEQS_GRP = 4
SEQS = 32


def draw_resets(key, part):
    key = jax.random.fold_in(key, 7)
    first_key = jax.random.fold_in(key, 1)
    second_key = jax.random.fold_in(key, 2)
    chance = jax.random.randint(first_key, (LENGTH, SEQS), 0, 48)
    marks = (chance == 0).astype(jnp.int32)
    keeper = jax.random.randint(second_key, (SEQS // SEQS_GRP,), 0, SEQS_GRP)
    columns = jnp.arange(SEQS, dtype=jnp.int32)
    clear = columns % SEQS_GRP == jnp.repeat(keeper, SEQS_GRP)
    rows_idx = jnp.arange(LENGTH, dtype=jnp.int32)
    forced = (rows_idx[:, None] == LENGTH // 2) & jnp.logical_not(clear)[None, :]
    marks = jnp.where(forced, 1, marks)
    return jnp.where(clear[None, :], 0, marks).astype(jnp.int32)


def draw_b_forget(key, part):
    key = jax.random.fold_in(key, 11)
    values = jax.random.uniform(key, (D,), jnp.float32, -1.0, 9.0)
    return values.astype(jnp.float32)


def block_scale(own_key, dims, split, smallest, top_value):
    level, own = 1.0, jax.random.fold_in(own_key, 6)
    for dim, blocks in split:
        draws = jnp.exp(jax.random.uniform(jax.random.fold_in(own, dim), (blocks,), jnp.float32, smallest / len(split), top_value / len(split)))
        level = level * jnp.repeat(draws, dims[dim] // blocks).reshape([-1 if axis == dim else 1 for axis in range(len(dims))])
    return level


def gaussian(rng, shape, width, bound, cuts=(), kind=jnp.bfloat16):
    array = jax.random.normal(rng, shape, jnp.float32) * width
    if len(cuts) > 0:
        array = block_scale(rng, shape, cuts, -0.22, 0.18) * array
    return jnp.clip(array, min=-bound, max=bound).astype(kind)


def setup_inputs(seed: int = 0) -> dict:
    arg_keys = jax.random.split(jax.random.key(seed), 11)
    return {
        "inputs": gaussian(arg_keys[0], (LENGTH, SEQS, D), 1.0, 6.0, ((0, 4), (1, 8))),
        "w_master": gaussian(arg_keys[1], (D, 3 * D), D ** -0.5, 0.125, (), jnp.float32),
        "v_forget": jnp.clip(jax.random.uniform(arg_keys[2], (D,), jnp.float32, -1.0, 1.0), -1.0, 1.0),
        "v_reset": jnp.clip(jax.random.uniform(arg_keys[3], (D,), jnp.float32, -1.0, 1.0), -1.0, 1.0),
        "b_forget": draw_b_forget(jax.random.fold_in(arg_keys[10], 71), 0),
        "b_reset": jnp.clip(jax.random.uniform(arg_keys[5], (D,), jnp.float32, -2.0, 2.0), -2.0, 2.0),
        "ln_gain": jnp.clip(1.0 + 0.1 * jax.random.normal(arg_keys[6], (D,), jnp.float32), 0.5, 1.5),
        "ln_shift": jnp.clip(jax.random.uniform(arg_keys[7], (D,), jnp.float32, -0.5, 0.5), -0.5, 0.5),
        "resets": draw_resets(jax.random.fold_in(arg_keys[10], 71), 0),
        "cotangent": gaussian(arg_keys[9], (LENGTH, SEQS, D), 1.0, 6.0, ((0, 4), (1, 8))),
    }


EPS = 1e-05

@jax.custom_vjp
def low(v):
    return lax.optimization_barrier(v.astype(jnp.bfloat16)).astype(jnp.float32)

@jax.custom_vjp
def low_back(v):
    return v

def low_keep(v):
    return (low(v), None)

def low_pass(kept, grad):
    return (grad,)

def back_keep(v):
    return (v, None)

def back_low(kept, grad):
    return (low(grad),)
low.defvjp(low_keep, low_pass)
low_back.defvjp(back_keep, back_low)

def layer(x_float, weight, v_forget, v_reset, b_forget, b_reset, ln_gain, ln_shift, retain):
    steps_n, seq_n, channels = x_float.shape
    average = lax.optimization_barrier(jnp.mean(x_float, -1, keepdims=True))
    centred = x_float - average
    inv_std = lax.rsqrt(lax.optimization_barrier(jnp.mean(centred * centred, -1, keepdims=True)) + EPS)
    normed = low(centred * inv_std * ln_gain + ln_shift)
    proj = jnp.dot(normed.reshape(steps_n * seq_n, channels), low(weight), precision=lax.Precision.HIGHEST, preferred_element_type=jnp.float32)
    proj = low_back(proj).reshape(steps_n, seq_n, 3 * channels)

    def advance(memory, pieces):
        candidate, pre_f, pre_r, x_step, retain_t = pieces
        prior = memory * retain_t[:, None]
        forget = jax.nn.sigmoid(pre_f + v_forget * prior + b_forget)
        rgate = jax.nn.sigmoid(pre_r + v_reset * prior + b_reset)
        fresh = forget * prior + (1.0 - forget) * candidate
        return (fresh, rgate * fresh + (1.0 - rgate) * x_step)
    pieces = (proj[..., :channels], proj[..., channels:2 * channels], proj[..., 2 * channels:], x_float, retain)
    start_mem = jnp.zeros((seq_n, channels), x_float.dtype)
    final, hidden = lax.scan(advance, start_mem, pieces)
    return (hidden, final)

def reference(inputs, w_master, v_forget, v_reset, b_forget, b_reset, ln_gain, ln_shift, resets, cotangent):
    retain = 1.0 - resets.astype(jnp.float32)
    groups = SEQS // SEQS_GRP
    params = (w_master, v_forget, v_reset, b_forget, b_reset, ln_gain, ln_shift)

    def one_group(sums, index):
        start = (index * SEQS_GRP).astype(jnp.int32)
        x_part = lax.dynamic_slice_in_dim(inputs, start, SEQS_GRP, 1).astype(jnp.float32)
        r_part = lax.dynamic_slice_in_dim(retain, start, SEQS_GRP, 1)
        g_part = lax.dynamic_slice_in_dim(cotangent, start, SEQS_GRP, 1).astype(jnp.float32)

        def apply_layer(x_float, weight, v_f, v_r, b_f, b_r, gain, shift):
            return layer(x_float, weight, v_f, v_r, b_f, b_r, gain, shift, r_part)
        hidden, pullback, final = jax.vjp(apply_layer, x_part, *params, has_aux=True)
        grads = pullback(g_part)
        sums = tuple((a + b for a, b in zip(sums, grads[1:])))
        return (sums, (hidden.astype(jnp.bfloat16), grads[0], final))
    start_sums = tuple((jnp.zeros(p.shape, jnp.float32) for p in params))
    sums, (hidden, x_grads, finals) = lax.scan(one_group, start_sums, jnp.arange(groups, dtype=jnp.int32))
    output = jnp.moveaxis(hidden, 0, 1).reshape(LENGTH, SEQS, D)
    input_grad = jnp.moveaxis(x_grads, 0, 1).reshape(LENGTH, SEQS, D)
    final_state = finals.reshape(SEQS, D)
    return (output, input_grad, sums[0], sums[1], sums[2], sums[3], sums[4], sums[5], sums[6], final_state)
```

```python
import functools
import math

import jax
import jax.numpy as jnp
from jax import lax
from jax.experimental import pallas as pl
from jax.experimental.pallas import tpu as pltpu
from jax.sharding import PartitionSpec as P

EPS = 1e-05
MESH = pl.DeviceIdType.MESH
F32 = jnp.float32
BF16 = jnp.bfloat16
LANES = 128
ROWS = 8
VMEM_BYTES = 62 * 1024 * 1024
COLS = 256
SLOTS = 4


def low_rows():
    return lax.broadcasted_iota(jnp.int32, (ROWS, LANES), 0) < ROWS // 2


def swap(value):
    return pltpu.roll(value, ROWS // 2, value.ndim - 2)


def pair_up(first, second):
    low = low_rows()
    return jnp.where(low, first, swap(second)), jnp.where(low, swap(first), second)


def unit_sum(value):
    total = jnp.sum(value, axis=0)
    total = total + swap(total)
    return jnp.sum(total, axis=-1, keepdims=True)


def spread_units(ref):
    low = low_rows()
    tiles = []
    for group in range(ref.shape[0] // 2):
        first = jnp.broadcast_to(ref[2 * group : 2 * group + 1, :], (ROWS, LANES))
        second = jnp.broadcast_to(ref[2 * group + 1 : 2 * group + 2, :], (ROWS, LANES))
        tiles.append(jnp.where(low, first, second))
    return jnp.stack(tiles, axis=0)


def project_kernel(
    x_ref,
    w_first_ref,
    w_odd_ref,
    w_next_ref,
    gain_ref,
    shift_ref,
    b_f_ref,
    resets_ref,
    proj_ref,
    normed,
    stats_ref,
    retain_ref,
    weight_even,
    weight_odd,
    bias,
    gain,
    shift,
):
    step = pl.program_id(0)
    positions, groups = stats_ref.shape[1], gain.shape[0]
    channels = groups * COLS
    span = groups * ROWS

    @pl.when(step == 0)
    def _():
        bias[0] = jnp.zeros((groups, ROWS, LANES), F32)
        bias[1] = spread_units(b_f_ref)
        gain[...] = spread_units(gain_ref)
        shift[...] = spread_units(shift_ref)
        weight_even[...] = w_first_ref[...].astype(BF16)
        retain = 1.0 - resets_ref[...].astype(F32)
        retain = jnp.concatenate([retain, retain], axis=0)
        for place in range(positions):
            retain_ref[place] = jnp.broadcast_to(retain[:, place : place + 1], (ROWS, LANES))

        def tokens_at(place):
            x = x_ref[pl.ds(pl.multiple_of(place * span, span), span), :]
            return x.astype(F32).reshape(groups, ROWS, LANES)

        @pl.loop(0, positions // 16)
        def _(turn):
            places = [turn * 16 + inner for inner in range(16)]
            means = [unit_sum(tokens_at(place)) * (1.0 / channels) for place in places]
            for place, mean in zip(places, means):
                stats_ref[0, place] = jnp.broadcast_to(mean, (ROWS, LANES))
            squares = []
            for place in places:
                centred = tokens_at(place) - stats_ref[0, place]
                squares.append(unit_sum(centred * centred) * (1.0 / channels))
            for place, square in zip(places, squares):
                stats_ref[1, place] = jnp.broadcast_to(lax.rsqrt(square + EPS), (ROWS, LANES))

        @pl.loop(0, positions // 4, unroll=2)
        def _(quad):
            tiles = []
            for inner in range(4):
                place = quad * 4 + inner
                normal = (tokens_at(place) - stats_ref[0, place]) * stats_ref[1, place]
                tiles.append(normal * gain[...] + shift[...])
            left0, right0 = pair_up(tiles[0], tiles[1])
            left1, right1 = pair_up(tiles[2], tiles[3])
            rows = pl.ds(pl.multiple_of(quad * 16, 16), 16)
            for group in range(groups):
                base = group * COLS
                left = jnp.concatenate([left0[group], left1[group]], axis=0)
                right = jnp.concatenate([right0[group], right1[group]], axis=0)
                normed[rows, base : base + LANES] = left.astype(BF16)
                normed[rows, base + LANES : base + COLS] = right.astype(BF16)

    def put(number, value):
        block = step * 2 + number
        offset = bias[block // groups, lax.rem(block, groups)]
        value = value.reshape(positions // 2, ROWS, COLS)
        even, odd = pair_up(value[:, :, :LANES], value[:, :, LANES:])
        proj_ref[0, number, :, 0] = (even + offset) * 0.5
        proj_ref[0, number, :, 1] = (odd + offset) * 0.5

    first = jnp.dot(normed[...], weight_even[...], preferred_element_type=F32)
    weight_odd[...] = w_odd_ref[...].astype(BF16)
    put(0, first)
    second = jnp.dot(normed[...], weight_odd[...], preferred_element_type=F32)
    weight_even[...] = w_next_ref[...].astype(BF16)
    put(1, second)


def project(x_packed, w_master, gain, shift, b_forget, resets, positions):
    channels = w_master.shape[0]
    groups = channels // COLS
    tokens = positions * 4
    steps = groups
    tile = (ROWS, LANES)

    def whole(shape):
        return pl.BlockSpec(shape, lambda step: (0,) * len(shape))

    def place(step):
        return 2 * step // groups, lax.rem(2 * step, groups) // 2, 0, 0, 0, 0

    return pl.pallas_call(
        project_kernel,
        grid=(steps,),
        in_specs=[
            whole(x_packed.shape),
            pl.BlockSpec((channels, COLS), lambda step: (0, 0)),
            pl.BlockSpec((channels, COLS), lambda step: (0, 2 * step + 1)),
            pl.BlockSpec(
                (channels, COLS), lambda step: (0, jnp.minimum(2 * step + 2, 2 * steps - 2))
            ),
            whole(gain.shape),
            whole(shift.shape),
            whole(b_forget.shape),
            whole(resets.shape),
        ],
        out_specs=[
            pl.BlockSpec((1, 2, positions // 2, 2) + tile, place),
            whole((tokens, channels)),
            whole((2, positions) + tile),
            whole((positions,) + tile),
        ],
        out_shape=[
            jax.ShapeDtypeStruct((2, groups, positions // 2, 2) + tile, F32),
            jax.ShapeDtypeStruct((tokens, channels), BF16),
            jax.ShapeDtypeStruct((2, positions) + tile, F32),
            jax.ShapeDtypeStruct((positions,) + tile, F32),
        ],
        scratch_shapes=[
            pltpu.VMEM((channels, COLS), BF16),
            pltpu.VMEM((channels, COLS), BF16),
            pltpu.VMEM((2, groups) + tile, F32),
            pltpu.VMEM((groups,) + tile, F32),
            pltpu.VMEM((groups,) + tile, F32),
        ],
        compiler_params=pltpu.CompilerParams(
            dimension_semantics=("arbitrary",), vmem_limit_bytes=VMEM_BYTES
        ),
        cost_estimate=pl.CostEstimate(
            flops=2 * tokens * channels * 2 * channels,
            bytes_accessed=4 * channels * 2 * channels + 4 * tokens * 2 * channels,
            transcendentals=0,
        ),
    )(x_packed, w_master, w_master, w_master, gain, shift, b_forget, resets)


def recur_kernel(
    proj_hbm,
    x_hbm,
    g_hbm,
    normed_hbm,
    w_hbm,
    retain_ref,
    v_f_raw,
    v_r_raw,
    b_r_raw,
    out_hbm,
    direct_hbm,
    dproj_hbm,
    sums_ref,
    final_ref,
    proj,
    state,
    fresh_part,
    x_ref,
    g_ref,
    out_stage,
    direct_stage,
    dz_r_stage,
    d_stage,
    later,
    first_d,
    incoming,
    leaving,
    final_in,
    v_f_ref,
    v_r_ref,
    b_r_ref,
    normed,
    w_block,
    weight,
    load_sem,
    token_sem,
    normed_sem,
    w_sem,
    out_sem,
    direct_sem,
    dz_r_sem,
    d_sem,
    carry_send,
    carry_recv,
    back_send,
    back_recv,
    final_send,
    final_recv,
    final_copy,
):
    groups, positions = proj.shape[1], proj.shape[2]
    channels = groups * COLS
    span = groups * ROWS
    count = lax.axis_size("sub")
    me = lax.axis_index("sub")
    last = count - 1
    stretch = 32
    stretches = positions // stretch

    def load(which, part):
        places = pl.ds(part * stretch, stretch)
        return pltpu.make_async_copy(
            proj_hbm.at[which, :, places], proj.at[which, :, places], load_sem.at[which, part]
        )

    early = me * 2 >= count
    ahead = jnp.where(early, jnp.where(me == last, groups, groups // 2), 0)

    def start_loads():
        for part in range(stretches):
            load(0, part).start()
            load(1, part).start()

    pl.when(jnp.logical_not(early))(start_loads)
    normed_copy = pltpu.make_async_copy(normed_hbm, normed, normed_sem)

    def w_copy(group):
        columns = pl.ds(pl.multiple_of(2 * channels + group * COLS, COLS), COLS)
        slot = lax.rem(group, 2)
        return pltpu.make_async_copy(w_hbm.at[:, columns], w_block.at[slot], w_sem.at[slot])

    chunk = 16
    chunks = positions // chunk

    def token_copies(turn):
        slot = lax.rem(turn, SLOTS)
        first = pl.multiple_of((chunks - 1 - turn) * (chunk * span), chunk * span)
        tile_rows = pl.ds(first, chunk * span)
        return (
            pltpu.make_async_copy(x_hbm.at[tile_rows], x_ref.at[slot], token_sem.at[0, slot]),
            pltpu.make_async_copy(g_hbm.at[tile_rows], g_ref.at[slot], token_sem.at[1, slot]),
        )

    def start_rest():
        normed_copy.start()
        w_copy(0).start()
        w_copy(1).start()
        for turn in range(SLOTS - 1):
            for copy in token_copies(turn):
                copy.start()

    pl.when(me > 0)(start_rest)

    barrier = pltpu.get_barrier_semaphore()
    for distance in range(1, count):
        pl.semaphore_signal(
            barrier,
            inc=1,
            device_id={"sub": lax.rem(me + distance, count)},
            device_id_type=MESH,
        )
    pl.semaphore_wait(barrier, count - 1)

    v_f_ref[...] = spread_units(v_f_raw)
    v_r_ref[...] = spread_units(v_r_raw)
    b_r_ref[...] = spread_units(b_r_raw)
    sums_ref[...] = jnp.zeros_like(sums_ref)
    later[...] = jnp.zeros_like(later)

    def carry_copy(target):
        return pltpu.make_async_remote_copy(
            src_ref=state.at[positions],
            dst_ref=state.at[0],
            send_sem=carry_send,
            recv_sem=carry_recv,
            device_id={"sub": target},
            device_id_type=MESH,
        )

    def back_copy(target):
        return pltpu.make_async_remote_copy(
            src_ref=leaving,
            dst_ref=incoming,
            send_sem=back_send,
            recv_sem=back_recv,
            device_id={"sub": target},
            device_id_type=MESH,
        )

    share = groups // count

    def final_piece(target):
        return pltpu.make_async_remote_copy(
            src_ref=state.at[positions, pl.ds(target * share, share)],
            dst_ref=final_in,
            send_sem=final_send.at[target],
            recv_sem=final_recv,
            device_id={"sub": target},
            device_id_type=MESH,
        )

    def put_reset(group, value):
        value = value.reshape(positions // 2, ROWS, COLS)
        even, odd = pair_up(value[:, :, :LANES], value[:, :, LANES:])
        both = jnp.stack([even, odd], axis=1).reshape(positions, ROWS, LANES)
        proj[2, group] = (both + b_r_ref[group]) * 0.5

    def project_group(group, carry):
        w_copy(group).wait()
        weight[...] = w_block[lax.rem(group, 2)].astype(BF16)

        @pl.when(group + 2 < groups)
        def _():
            w_copy(group + 2).start()

        put_reset(group, jnp.dot(normed[...], weight[...], preferred_element_type=F32))
        return carry

    @pl.when(early)
    def _():
        normed_copy.wait()
        start_loads()
        lax.fori_loop(0, ahead, project_group, 0)

    @pl.when(me == 0)
    def _():
        state[0] = jnp.zeros_like(state[0])

    @pl.when(me > 0)
    def _():
        carry_copy(me).wait_recv()

    v_f_half = v_f_ref[...] * 0.5

    def advance(place, carry):
        retain = retain_ref[place]
        cand_half = proj[0, :, place]
        gate = jnp.tanh(proj[1, :, place] + (v_f_half * retain) * carry)
        prior_half = carry * (retain * 0.5)
        fresh = (prior_half + cand_half) + gate * (prior_half - cand_half)
        state[place + 1] = fresh
        return fresh

    def advance_part(part, carry):
        load(0, part).wait()
        load(1, part).wait()
        return lax.fori_loop(
            0, stretch, lambda inner, c: advance(part * stretch + inner, c), carry, unroll=16
        )

    lax.fori_loop(0, stretches, advance_part, state[0])

    @pl.when(me < last)
    def _():
        carry_copy(me + 1).start()

    @pl.when(me == last)
    def _():
        for target in range(count - 1):
            final_piece(target).start()
        own = pltpu.make_async_copy(
            state.at[positions, pl.ds((count - 1) * share, share)], final_in, final_copy
        )
        own.start()
        own.wait()

    pl.when(me == 0)(start_rest)
    pl.when(jnp.logical_not(early))(normed_copy.wait)
    lax.fori_loop(ahead, groups, project_group, 0)

    def out_copies(index, slot):
        tile_rows = pl.ds(pl.multiple_of(index * (chunk * span), chunk * span), chunk * span)
        token_rows = pl.ds(pl.multiple_of(index * (chunk * 4), chunk * 4), chunk * 4)
        return (
            pltpu.make_async_copy(out_stage.at[slot], out_hbm.at[tile_rows], out_sem.at[slot]),
            pltpu.make_async_copy(
                direct_stage.at[slot],
                direct_hbm.at[pl.ds(index * chunk, chunk)],
                direct_sem.at[slot],
            ),
            pltpu.make_async_copy(
                dz_r_stage.at[slot],
                dproj_hbm.at[token_rows, pl.ds(2 * channels, channels)],
                dz_r_sem.at[slot],
            ),
        )

    def to_rows(stage, slot, base_row, column, by_place):
        left0, right0 = pair_up(by_place[0], by_place[1])
        left1, right1 = pair_up(by_place[2], by_place[3])
        rows = pl.ds(base_row, 16)
        for group in range(2):
            base = column + group * COLS
            left = jnp.concatenate([left0[group], left1[group]], axis=0)
            right = jnp.concatenate([right0[group], right1[group]], axis=0)
            stage[slot, rows, pl.ds(pl.multiple_of(base, LANES), LANES)] = left.astype(BF16)
            stage[slot, rows, pl.ds(pl.multiple_of(base + LANES, LANES), LANES)] = right.astype(
                BF16
            )

    def gates(index, slot, block, pair):
        duo = pl.ds(pair * 2, 2)
        v_f = v_f_ref[duo]
        v_r = v_r_ref[duo]
        v_f_h = v_f * 0.5
        v_r_h = v_r * 0.5
        next_d = later[duo]
        sum_r = sums_ref[3, duo]
        sum_rp = sums_ref[1, duo]
        dz_r_of = [None] * 8
        start = index * chunk + block * 8
        for inner in reversed(range(8)):
            place = start + inner
            inside = block * 8 + inner
            tile = pl.ds(pl.multiple_of(inside * span + pair * 16, 16), 16)
            retain = retain_ref[place]
            x = x_ref[slot, tile, :].astype(F32).reshape(2, ROWS, LANES)
            g = g_ref[slot, tile, :].astype(F32).reshape(2, ROWS, LANES)
            cand = 2.0 * proj[0, duo, place]
            prior = state[place, duo] * retain
            fresh = state[place + 1, duo]
            forget = 0.5 + 0.5 * jnp.tanh(proj[1, duo, place] + v_f_h * prior)
            rgate = 0.5 + 0.5 * jnp.tanh(proj[2, duo, place] + v_r_h * prior)
            keep = 1.0 - forget
            slope = (prior - cand) * (forget * keep)
            apart = fresh - x
            hidden = x + rgate * apart
            g_r = g * rgate
            direct = g - g_r
            dz_r = (g_r * apart) * (1.0 - rgate)
            factor = retain * (forget + slope * v_f)
            here_d = (retain * v_r) * dz_r
            proj[0, duo, place] = slope
            proj[1, duo, place] = factor
            proj[2, duo, place] = g_r + next_d
            fresh_part[duo, place] = keep
            next_d = here_d
            sum_r = sum_r + dz_r
            sum_rp = sum_rp + dz_r * prior
            dz_r_of[inner] = dz_r
            out_stage[slot, tile, :] = hidden.reshape(16, LANES).astype(BF16)
            direct_stage[slot, inside, duo] = direct
        later[duo] = next_d
        sums_ref[3, duo] = sum_r
        sums_ref[1, duo] = sum_rp
        for quad in range(2):
            to_rows(
                dz_r_stage,
                slot,
                pl.multiple_of(block * 32 + quad * 16, 16),
                pair * (2 * COLS),
                dz_r_of[quad * 4 : quad * 4 + 4],
            )

    @pl.loop(0, chunks)
    def _(turn):
        index = chunks - 1 - turn
        slot = lax.rem(turn, SLOTS)

        @pl.when(turn >= SLOTS)
        def _():
            for copy in out_copies(index + SLOTS, slot):
                copy.wait()

        for copy in token_copies(turn):
            copy.wait()

        @pl.when(turn + SLOTS - 1 < chunks)
        def _():
            for copy in token_copies(turn + SLOTS - 1):
                copy.start()

        @pl.loop(0, groups // 2)
        def _(pair):
            gates(index, slot, 1, pair)
            gates(index, slot, 0, pair)

        for copy in out_copies(index, slot):
            copy.start()

    first_d[...] = later[...]
    middle = (me > 0) & (me < last)
    block_maps = positions // 8

    def map_rows(block):
        return pl.ds(pl.multiple_of(block * span, span), span)

    @pl.when(middle)
    def _():
        @pl.loop(0, block_maps)
        def _(block):
            top = block * 8 + 7
            slope = proj[1, :, top]
            constant = slope * proj[2, :, top]
            for inner in range(1, 8):
                factor = proj[1, :, top - inner]
                constant = factor * (proj[2, :, top - inner] + constant)
                slope = factor * slope
            w_block[0, map_rows(block), :LANES] = slope.reshape(span, LANES)
            w_block[0, map_rows(block), LANES:] = constant.reshape(span, LANES)

    @pl.when(me == last)
    def _():
        incoming[...] = jnp.zeros_like(incoming)

    @pl.when(me < last)
    def _():
        back_copy(me).wait_recv()

    @pl.when(middle)
    def _():
        def skip(turn, carried):
            block = block_maps - 1 - turn
            slope = w_block[0, map_rows(block), :LANES].reshape(groups, ROWS, LANES)
            constant = w_block[0, map_rows(block), LANES:].reshape(groups, ROWS, LANES)
            return constant + slope * carried

        leaving[...] = first_d[...] + lax.fori_loop(
            0, block_maps, skip, incoming[...], unroll=8
        )

    @pl.when(me == last)
    def _():
        def retreat(turn, carried):
            place = positions - 1 - turn
            return proj[1, :, place] * (proj[2, :, place] + carried)

        leaving[...] = first_d[...] + lax.fori_loop(
            0, positions, retreat, incoming[...], unroll=16
        )

    @pl.when(me > 0)
    def _():
        back_copy(me - 1).start()

    def d_copy(index, slot):
        token_rows = pl.ds(pl.multiple_of(index * (chunk * 4), chunk * 4), chunk * 4)
        return pltpu.make_async_copy(
            d_stage.at[slot], dproj_hbm.at[token_rows, pl.ds(0, 2 * channels)], d_sem.at[slot]
        )

    def finish(index, slot, block, pair):
        duo = pl.ds(pair * 2, 2)
        carried = incoming[duo]
        sum_f = sums_ref[2, duo]
        sum_fp = sums_ref[0, duo]
        cand_of, dz_f_of = [None] * 8, [None] * 8
        for inner in reversed(range(8)):
            place = index * chunk + block * 8 + inner
            summed = proj[2, duo, place] + carried
            carried = proj[1, duo, place] * summed
            prior = state[place, duo] * retain_ref[place]
            dz_f = summed * proj[0, duo, place]
            sum_f = sum_f + dz_f
            sum_fp = sum_fp + dz_f * prior
            cand_of[inner] = summed * fresh_part[duo, place]
            dz_f_of[inner] = dz_f
        incoming[duo] = carried
        sums_ref[2, duo] = sum_f
        sums_ref[0, duo] = sum_fp
        for quad in range(2):
            row = pl.multiple_of(block * 32 + quad * 16, 16)
            column = pair * (2 * COLS)
            to_rows(d_stage, slot, row, column, cand_of[quad * 4 : quad * 4 + 4])
            to_rows(d_stage, slot, row, channels + column, dz_f_of[quad * 4 : quad * 4 + 4])

    @pl.loop(0, chunks)
    def _(turn):
        index = chunks - 1 - turn
        slot = lax.rem(turn, SLOTS)

        @pl.when(turn >= SLOTS)
        def _():
            d_copy(index + SLOTS, slot).wait()

        @pl.loop(0, groups // 2)
        def _(pair):
            finish(index, slot, 1, pair)
            finish(index, slot, 0, pair)

        d_copy(index, slot).start()

    for turn in range(chunks - SLOTS, chunks):
        for copy in out_copies(chunks - 1 - turn, turn % SLOTS):
            copy.wait()
        d_copy(chunks - 1 - turn, turn % SLOTS).wait()

    @pl.when(me < last)
    def _():
        carry_copy(me + 1).wait_send()
        final_piece(me).wait_recv()

    @pl.when(me == last)
    def _():
        for target in range(count - 1):
            final_piece(target).wait_send()

    @pl.when(me > 0)
    def _():
        back_copy(me - 1).wait_send()

    final_ref[...] = final_in[...]


def recur(proj, x_packed, g_packed, normed, w_master, retain, v_f, v_r, b_r, sub_count):
    groups, positions = proj.shape[1], proj.shape[2]
    channels = groups * COLS
    tokens = positions * 4
    span = groups * ROWS
    chunk = 16
    tile = (ROWS, LANES)
    share = groups // sub_count
    anywhere = pl.BlockSpec(memory_space=pltpu.HBM)
    local = pl.BlockSpec(memory_space=pltpu.VMEM)
    dma = pltpu.SemaphoreType.DMA
    return pl.pallas_call(
        recur_kernel,
        in_specs=[anywhere] * 5 + [local] * 4,
        out_specs=[anywhere] * 3 + [local] * 2,
        out_shape=[
            jax.ShapeDtypeStruct(x_packed.shape, BF16),
            jax.ShapeDtypeStruct((positions, groups) + tile, F32),
            jax.ShapeDtypeStruct((tokens, 3 * channels), BF16),
            jax.ShapeDtypeStruct((4, groups) + tile, F32),
            jax.ShapeDtypeStruct((share,) + tile, F32),
        ],
        scratch_shapes=[
            pltpu.VMEM((3, groups, positions) + tile, F32),
            pltpu.VMEM((positions + 1, groups) + tile, F32),
            pltpu.VMEM((groups, positions) + tile, F32),
            pltpu.VMEM((SLOTS, chunk * span, LANES), BF16),
            pltpu.VMEM((SLOTS, chunk * span, LANES), BF16),
            pltpu.VMEM((SLOTS, chunk * span, LANES), BF16),
            pltpu.VMEM((SLOTS, chunk, groups) + tile, F32),
            pltpu.VMEM((SLOTS, chunk * 4, channels), BF16),
            pltpu.VMEM((SLOTS, chunk * 4, 2 * channels), BF16),
            pltpu.VMEM((groups,) + tile, F32),
            pltpu.VMEM((groups,) + tile, F32),
            pltpu.VMEM((groups,) + tile, F32),
            pltpu.VMEM((groups,) + tile, F32),
            pltpu.VMEM((share,) + tile, F32),
            pltpu.VMEM((groups,) + tile, F32),
            pltpu.VMEM((groups,) + tile, F32),
            pltpu.VMEM((groups,) + tile, F32),
            pltpu.VMEM((tokens, channels), BF16),
            pltpu.VMEM((2, channels, COLS), F32),
            pltpu.VMEM((channels, COLS), BF16),
            dma((2, positions // 32)),
            dma((2, SLOTS)),
            dma,
            dma((2,)),
            dma((SLOTS,)),
            dma((SLOTS,)),
            dma((SLOTS,)),
            dma((SLOTS,)),
            dma,
            dma,
            dma,
            dma,
            dma((sub_count,)),
            dma,
            dma,
        ],
        compiler_params=pltpu.CompilerParams(
            collective_id=0, has_side_effects=True, vmem_limit_bytes=VMEM_BYTES
        ),
        cost_estimate=pl.CostEstimate(
            flops=(100 + 2 * channels) * tokens * channels,
            bytes_accessed=60 * tokens * channels,
            transcendentals=3 * tokens * channels,
        ),
    )(proj, x_packed, g_packed, normed, w_master, retain, v_f, v_r, b_r)


class Axis:

    def __init__(self, name, stride, size):
        self.name, self.stride, self.size = name, stride, size

    def place(self):
        return lax.rem(lax.axis_index(self.name) // self.stride, self.size)

    def device(self, shift):
        return {self.name: lax.axis_index(self.name) + shift * self.stride}


def lines(name, size, stride):
    found = []
    while size > 1:
        part = 4 if size % 4 == 0 else 2 if size % 2 == 0 else size
        found.append(Axis(name, stride, part))
        stride, size = stride * part, size // part
    return found


def routes(dp_count, sub_count):
    core = lines("sub", 2, 1)
    across = lines("sub", sub_count // 2, 2)
    slow = 4 if dp_count % 4 == 0 else 1
    long = lines("dp", slow, dp_count // slow)
    fast = lines("dp", dp_count // slow, 1)
    return core + across + long + fast, core + fast + long + across, core + across + fast + long


class Phase:

    def __init__(self, kind, axis, step, level, slots):
        self.kind, self.axis, self.step, self.level, self.slots = kind, axis, step, level, slots


def plan(route, rows, slots):
    levels, phases, size = [], [], rows
    for axis in route:
        levels.append((axis, size))
        size //= axis.size
    for level, (axis, _) in enumerate(levels):
        for step in range(1, axis.size):
            phases.append(Phase("sum", axis, step, level, 2 if axis.size == 2 else slots))
    for level, (axis, _) in reversed(list(enumerate(levels))):
        for step in range(1, axis.size):
            phases.append(Phase("give", axis, step, level, 2 if axis.size == 2 else slots))
    return levels, phases


class Stream:

    def __init__(self, levels, phases, acc, landing, send_sem, recv_sem):
        self.levels, self.phases, self.acc, self.landing = levels, phases, acc, landing
        self.send_sem, self.recv_sem = send_sem, recv_sem
        self.offsets, self.places = [], []
        offset = 0
        for axis, size in levels:
            place = axis.place()
            self.places.append(place)
            self.offsets.append(offset)
            offset = offset + place * (size // axis.size)

    def region(self, slot, level, piece):
        axis, size = self.levels[level]
        rows = size // axis.size
        start = pl.multiple_of(self.offsets[level] + piece * rows, ROWS)
        return self.acc.at[slot, pl.ds(start, rows)]

    def transfers(self, number):
        phase = self.phases[number]
        place, size, step = self.places[phase.level], phase.axis.size, phase.step
        if size == 2:
            shift = 1 - 2 * place
            if phase.kind == "sum":
                return [(None, 1 - place, shift, 0)], [(None, place, shift, 0)]
            return [(None, place, shift, 0)], [(None, 1 - place, shift, 0)]
        sends, receives = [], []
        for way in range(2):
            shift = 1 if way == 0 else -1
            seen = place if way == 0 else size - 1 - place

            def actual(piece, way=way):
                return piece if way == 0 else size - 1 - piece

            if phase.kind == "sum":
                sends.append(
                    (
                        (seen <= size - 2) & (seen + 1 <= step),
                        actual(size - step + seen),
                        shift,
                        way,
                    )
                )
                receives.append(
                    ((seen >= 1) & (seen <= step), actual(size - step + seen - 1), -shift, way)
                )
            else:
                sends.append(
                    ((seen <= size - 2) & (seen + 1 >= step), actual(seen - step + 1), shift, way)
                )
                receives.append(((seen >= 1) & (seen >= step), actual(seen - step), -shift, way))
        return sends, receives

    def copy(self, number, chunk, slot, piece, shift, way):
        phase = self.phases[number]
        source = self.region(slot, phase.level, piece)
        landing = self.landing[number]
        target = landing.at[way, lax.rem(chunk, phase.slots)]
        return pltpu.make_async_remote_copy(
            src_ref=source,
            dst_ref=target,
            send_sem=self.send_sem.at[number, way],
            recv_sem=self.recv_sem.at[number, way, lax.rem(chunk, 4)],
            device_id=phase.axis.device(shift),
            device_id_type=MESH,
        )

    def start(self, number, chunk, slot):
        for condition, piece, shift, way in self.transfers(number)[0]:
            run = self.copy(number, chunk, slot, piece, shift, way).start
            if condition is None:
                run()
            else:
                pl.when(condition)(run)

    def finish(self, number, chunk, slot):
        phase = self.phases[number]
        sends, receives = self.transfers(number)
        for condition, piece, shift, way in receives:

            def take(piece=piece, shift=shift, way=way):
                self.copy(number, chunk, slot, piece, shift, way).wait_recv()
                place = self.region(slot, phase.level, piece)
                landed = self.landing[number][way, lax.rem(chunk, phase.slots)]
                place[...] = place[...] + landed if phase.kind == "sum" else landed

            if condition is None:
                take()
            else:
                pl.when(condition)(take)
        for condition, piece, shift, way in sends:
            done = self.copy(number, chunk, slot, piece, shift, way).wait_send
            if condition is None:
                done()
            else:
                pl.when(condition)(done)


def gradient_kernel(shape, *refs):
    plans, timing, rings, chunk_rows = shape
    (
        normed_hbm,
        dproj_hbm,
        w_hbm,
        x_hbm,
        stats_hbm,
        direct_hbm,
        gain_raw,
        gate_sums_ref,
        w_grad_hbm,
        input_grad_hbm,
        *rest,
    ) = refs
    accs, rest = rest[: len(plans)], rest[len(plans) :]
    (
        gain_ref,
        normed,
        turned,
        left_block,
        through_block,
        w_block,
        d_normed,
        norm_sums,
        x_stage,
        stats_stage,
        direct_stage,
        grad_stage,
        normed_sem,
        left_sem,
        through_sem,
        w_sem,
        in_sem,
        grad_sem,
        *rest,
    ) = rest
    sems, landings = rest[: 3 * len(plans)], list(rest[3 * len(plans) :])
    groups = gain_raw.shape[0] // 2
    channels = groups * COLS
    tokens = turned.shape[1]
    positions = tokens // 4
    span = groups * ROWS
    blocks = 3 * groups
    row_blocks = channels // chunk_rows
    batch = 16
    batches = positions // batch

    def normed_copy(part):
        columns = pl.ds(pl.multiple_of(part * chunk_rows, chunk_rows), chunk_rows)
        return pltpu.make_async_copy(
            normed_hbm.at[:, columns], normed.at[:, columns], normed_sem.at[part]
        )

    for part in range(row_blocks):
        normed_copy(part).start()

    def column_block(block):
        return pl.ds(pl.multiple_of(block * COLS, COLS), COLS)

    def left_copy(block):
        slot = lax.rem(block, 2)
        return pltpu.make_async_copy(
            dproj_hbm.at[:, column_block(block)], left_block.at[slot], left_sem.at[slot]
        )

    wide = 3 * COLS
    units_count = blocks // 3 * groups
    w_slots = 4

    def wide_columns(triple):
        return pl.ds(pl.multiple_of(triple * wide, wide), wide)

    def through_copy(triple):
        slot = lax.rem(triple, 2)
        return pltpu.make_async_copy(
            dproj_hbm.at[:, wide_columns(triple)], through_block.at[slot], through_sem.at[slot]
        )

    def w_copy(unit):
        rows = pl.ds(pl.multiple_of(lax.rem(unit, groups) * COLS, COLS), COLS)
        slot = lax.rem(unit, w_slots)
        return pltpu.make_async_copy(
            w_hbm.at[rows, wide_columns(unit // groups)], w_block.at[slot], w_sem.at[slot]
        )

    left_copy(0).start()
    through_copy(0).start()
    for unit in range(w_slots - 1):
        w_copy(unit).start()

    streams = []
    for number, (levels, phases) in enumerate(plans):
        send, recv = sems[3 * number], sems[3 * number + 1]
        own = {}
        for index in range(len(phases)):
            own[index] = landings.pop(0)
        streams.append(Stream(levels, phases, accs[number], own, send, recv))

    barrier = pltpu.get_barrier_semaphore()
    expected = 0
    for axis, _ in plans[0][0]:
        place = axis.place()
        if axis.size == 2:
            pl.semaphore_signal(
                barrier, inc=1, device_id=axis.device(1 - 2 * place), device_id_type=MESH
            )
            expected = expected + 1
        else:
            for condition, shift in ((place < axis.size - 1, 1), (place > 0, -1)):

                @pl.when(condition)
                def _(axis=axis, shift=shift):
                    pl.semaphore_signal(
                        barrier, inc=1, device_id=axis.device(shift), device_id_type=MESH
                    )

                expected = expected + jnp.where(condition, 1, 0)
    gain_ref[...] = spread_units(gain_raw)
    norm_sums[...] = jnp.zeros_like(norm_sums)
    count = len(plans[0][1])

    def result_copy(number, chunk, slot):
        index = timing.index(number, chunk)
        rows = pl.ds(pl.multiple_of(lax.rem(index, row_blocks) * chunk_rows, chunk_rows), chunk_rows)
        return pltpu.make_async_copy(
            accs[number].at[slot],
            w_grad_hbm.at[rows, column_block(index // row_blocks)],
            sems[3 * number + 2].at[slot],
        )

    first_kept = kept_chunks(timing, rings, row_blocks)[1]

    def deliver(number, chunk, slot, act):
        @pl.when(
            (chunk < timing.chunks[number])
            & (timing.index(number, chunk) < first_kept * row_blocks)
        )
        def _():
            act(result_copy(number, chunk, slot))

    part = min(1024, chunk_rows)

    def prepare(index, first, block):
        @pl.when((block == 0) & (index > 0))
        def _():
            normed_copy(index).wait()

            @pl.loop(0, chunk_rows // COLS)
            def _(piece):
                units = pl.ds(pl.multiple_of(first + piece * COLS, COLS), COLS)
                turned[units, :] = normed[:, units].T

        @pl.when(lax.rem(index, row_blocks) == 0)
        def _():
            left_copy(block).wait()

            @pl.when(block + 1 < blocks)
            def _():
                left_copy(block + 1).start()

    def multiply(first, rows_count, block):
        rows = pl.ds(pl.multiple_of(first, rows_count), rows_count)
        return jnp.dot(
            turned[rows, :], left_block[lax.rem(block, 2)], preferred_element_type=F32
        )

    together = row_blocks % 2 == 0 and 2 * chunk_rows <= part

    def compute(number, chunk, slot):
        index = timing.index(number, chunk)
        first = lax.rem(index, row_blocks) * chunk_rows
        block = index // row_blocks
        if together:

            @pl.when(block == 0)
            def _():
                prepare(index, first, block)
                accs[number][slot] = multiply(first, chunk_rows, block)

            if number == 0:
                @pl.when(block > 0)
                def _():
                    prepare(index, first, block)
                    value = multiply(first, 2 * chunk_rows, block)
                    accs[0][slot] = value[:chunk_rows]
                    accs[1][slot] = value[chunk_rows:]

            return
        prepare(index, first, block)

        @pl.loop(0, chunk_rows // part)
        def _(piece):
            accs[number][slot, pl.ds(pl.multiple_of(piece * part, part), part)] = multiply(
                first + piece * part, part, block
            )

    def gather_sums(slot):
        acc = accs[timing.sums_stream]
        acc[slot] = jnp.zeros((chunk_rows, COLS), F32)
        for index in range(6):
            for group in range(groups):
                source = gate_sums_ref[index, group] if index < 4 else norm_sums[index - 4, group]
                row = (index * groups + group) * ROWS
                acc[slot, row : row + ROWS, :LANES] = source

    def event(tick, number, turn):
        first, spacing = timing.starts[number], timing.spacings[number]
        since = tick - turn - first
        chunk = since // spacing
        slot = lax.rem(chunk, rings[number])
        total = timing.chunks[number] + timing.sums(number)
        due = (since >= 0) & (chunk < total)
        if spacing > 1:
            due = due & (lax.rem(since, spacing) == 0)

        @pl.when(due)
        def _():
            stream = streams[number]
            if turn == 0:
                if timing.sums(number):

                    @pl.when(chunk < timing.chunks[number])
                    def _():
                        compute(number, chunk, slot)

                    @pl.when(chunk == timing.chunks[number])
                    def _():
                        gather_sums(slot)
                else:
                    compute(number, chunk, slot)
            elif turn <= count:
                stream.finish(turn - 1, chunk, slot)
            if turn < count:
                stream.start(turn, chunk, slot)
            if turn == count:
                deliver(number, chunk, slot, lambda copy: copy.start())
            if turn == count + 1:
                deliver(number, chunk, slot, lambda copy: copy.wait())

    def through_weight(unit, carry):
        triple, piece = unit // groups, lax.rem(unit, groups)

        @pl.when(piece == 0)
        def _():
            through_copy(triple).wait()

            @pl.when(triple + 1 < blocks // 3)
            def _():
                through_copy(triple + 1).start()

        @pl.when(unit + w_slots - 1 < units_count)
        def _():
            w_copy(unit + w_slots - 1).start()

        w_copy(unit).wait()
        units = pl.ds(pl.multiple_of(piece * COLS, COLS), COLS)
        value = lax.dot_general(
            through_block[lax.rem(triple, 2)],
            w_block[lax.rem(unit, w_slots)].astype(BF16),
            (((1,), (1,)), ((), ())),
            preferred_element_type=F32,
        )

        @pl.when(triple == 0)
        def _():
            d_normed[:, units] = value

        @pl.when(triple > 0)
        def _():
            d_normed[:, units] += value

        return carry

    def in_copies(index):
        slot = lax.rem(index, 2)
        tile_rows = pl.ds(pl.multiple_of(index * (batch * span), batch * span), batch * span)
        places = pl.ds(index * batch, batch)
        return (
            pltpu.make_async_copy(x_hbm.at[tile_rows], x_stage.at[slot], in_sem.at[0, slot]),
            pltpu.make_async_copy(
                stats_hbm.at[:, places], stats_stage.at[slot], in_sem.at[1, slot]
            ),
            pltpu.make_async_copy(direct_hbm.at[places], direct_stage.at[slot], in_sem.at[2, slot]),
        )

    def grad_copy(index):
        slot = lax.rem(index, 2)
        return pltpu.make_async_copy(
            grad_stage.at[slot], input_grad_hbm.at[pl.ds(index * batch, batch)], grad_sem.at[slot]
        )

    def normal_at(slot, place):
        x = x_stage[slot, pl.ds(pl.multiple_of(place * span, span), span), :]
        x = x.astype(F32).reshape(groups, ROWS, LANES)
        return (x - stats_stage[slot, 0, place]) * stats_stage[slot, 1, place]

    def through_norm(index):
        slot = lax.rem(index, 2)
        for copy in in_copies(index):
            copy.wait()

        @pl.when(index + 1 < batches)
        def _():
            for copy in in_copies(index + 1):
                copy.start()

        @pl.when(index >= 2)
        def _():
            grad_copy(index - 2).wait()

        @pl.loop(0, batch // 8)
        def _(turn):
            places = [turn * 8 + inner for inner in range(8)]
            halves = []
            for pair in range(4):
                row = index * (batch * 4) + turn * 32 + pair * ROWS
                rows = pl.ds(pl.multiple_of(row, ROWS), ROWS)
                left = [d_normed[rows, g * COLS : g * COLS + LANES] for g in range(groups)]
                right = [d_normed[rows, g * COLS + LANES : (g + 1) * COLS] for g in range(groups)]
                grads = pair_up(jnp.stack(left, axis=0), jnp.stack(right, axis=0))
                for place, grad in zip(places[2 * pair : 2 * pair + 2], grads):
                    grad_stage[slot, place] = grad
                    hat = grad * gain_ref[...]
                    both = hat * normal_at(slot, place)
                    halves.append((jnp.sum(hat, axis=0), jnp.sum(both, axis=0)))
            means = []
            for pair in halves:
                wholes = [jnp.sum(half + swap(half), axis=-1, keepdims=True) for half in pair]
                means.append([whole * (1.0 / channels) for whole in wholes])
            total_normal, total = norm_sums[0], norm_sums[1]
            for place, (mean_hat, mean_both) in zip(places, means):
                grad = grad_stage[slot, place]
                normal = normal_at(slot, place)
                hat = grad * gain_ref[...]
                layer = stats_stage[slot, 1, place] * (hat - mean_hat - normal * mean_both)
                grad_stage[slot, place] = direct_stage[slot, place] + layer
                total_normal = total_normal + grad * normal
                total = total + grad
            norm_sums[0] = total_normal
            norm_sums[1] = total

        grad_copy(index).start()

    main = timing.sums_tick
    at_once = 2
    norm_from = main - batches // at_once
    ticks = timing.last_tick + count + 2

    normed_copy(0).wait()

    @pl.loop(0, chunk_rows // COLS)
    def _(piece):
        units = pl.ds(pl.multiple_of(piece * COLS, COLS), COLS)
        turned[units, :] = normed[:, units].T

    pl.semaphore_wait(barrier, expected)

    @pl.loop(0, ticks)
    def _(tick):
        for turn in reversed(range(count + 2)):
            for number in range(len(plans)):
                event(tick, number, turn)

        @pl.when(tick < norm_from)
        def _():
            begin = (tick * units_count) // norm_from
            end = ((tick + 1) * units_count) // norm_from
            lax.fori_loop(begin, end, through_weight, 0)

        @pl.when(tick == norm_from - 1)
        def _():
            for copy in in_copies(0):
                copy.start()

        @pl.when((tick >= norm_from) & (tick < main))
        def _():
            for inner in range(at_once):
                through_norm((tick - norm_from) * at_once + inner)

    for index in range(max(batches - 2, 0), batches):
        grad_copy(index).wait()


class Timing:

    def __init__(self, total, spacing, third):
        self.third = third
        if third:
            self.starts, self.spacings = (0, 0, third // 2), (1, 1, third)
            done, tick, counts = 0, 0, [0, 0, 0]
            while done < total:
                for number in range(3):
                    if done < total and tick % self.spacings[number] == self.starts[number]:
                        counts[number] += 1
                        done += 1
                tick += 1
            self.chunks = tuple(counts)
        else:
            self.starts, self.spacings = (0, spacing // 2), (spacing, spacing)
            self.chunks = (total - total // 2, total // 2)
        self.sums_stream = len(self.chunks) - 1 if third else 0
        self.sums_tick = self.tick(self.sums_stream, self.chunks[self.sums_stream])
        ends = [self.tick(n, count - 1) for n, count in enumerate(self.chunks)]
        self.last_tick = max(ends + [self.sums_tick])

    def tick(self, number, chunk):
        return self.starts[number] + chunk * self.spacings[number]

    def sums(self, number):
        return 1 if number == self.sums_stream else 0

    def index(self, number, chunk):
        if not self.third:
            return chunk * 2 + number
        if number == 2:
            return chunk * (2 * self.third + 1) + 2 * self.starts[2] + 2
        return chunk * 2 + (chunk + self.third - self.starts[2] - 1) // self.third + number


def gradient_plan(channels, dp_count, sub_count):
    devices = dp_count * sub_count
    chunk_rows = min(channels, max(512, ROWS * devices))
    total = 3 * (channels // COLS) * (channels // chunk_rows)
    both = routes(dp_count, sub_count)
    count = 2 * sum(axis.size - 1 for axis in both[0])
    stay = count + 2
    most = 16 * 1024 * 1024
    spacing = 1
    while -(-stay // spacing) * 2 * chunk_rows * COLS * 4 > most:
        spacing += 1
    third = 0
    timing = Timing(total, spacing, third)
    rings = tuple(-(-stay // step) for step in timing.spacings)
    plans = tuple(
        plan(route, chunk_rows, 4 if spacing == 1 else 2) for route in both[: len(rings)]
    )
    return plans, timing, rings, chunk_rows


def gradients(shape, normed, dproj, w_master, x_packed, stats, direct, gain, gate_sums):
    plans, timing, rings, chunk_rows = shape
    tokens, channels = normed.shape
    groups = channels // COLS
    positions = tokens // 4
    span = groups * ROWS
    blocks = 3 * groups
    batch = 16
    count = len(plans[0][1])
    tile = (ROWS, LANES)
    anywhere = pl.BlockSpec(memory_space=pltpu.HBM)
    local = pl.BlockSpec(memory_space=pltpu.VMEM)
    dma = pltpu.SemaphoreType.DMA
    landing = []
    for levels, phases in plans:
        for phase in phases:
            ways = 1 if phase.axis.size == 2 else 2
            rows = levels[phase.level][1] // phase.axis.size
            landing.append(pltpu.VMEM((ways, phase.slots, rows, COLS), F32))
    buffers = [
        pltpu.VMEM((groups,) + tile, F32),
        pltpu.VMEM((tokens, channels), BF16),
        pltpu.VMEM((channels, tokens), BF16),
        pltpu.VMEM((2, tokens, COLS), BF16),
        pltpu.VMEM((2, tokens, 3 * COLS), BF16),
        pltpu.VMEM((4, COLS, 3 * COLS), F32),
        pltpu.VMEM((tokens, channels), F32),
        pltpu.VMEM((2, groups) + tile, F32),
        pltpu.VMEM((2, batch * span, LANES), BF16),
        pltpu.VMEM((2, 2, batch) + tile, F32),
        pltpu.VMEM((2, batch, groups) + tile, F32),
        pltpu.VMEM((2, batch, groups) + tile, F32),
    ]
    semaphores = [
        dma((channels // chunk_rows,)),
        dma((2,)),
        dma((2,)),
        dma((4,)),
        dma((3, 2)),
        dma((2,)),
    ]
    for ring in rings:
        semaphores += [dma((count, 2)), dma((count, 2, 4)), dma((ring,))]
    held = sum(math.prod(b.shape) * jnp.dtype(b.dtype).itemsize for b in buffers + landing)
    return pl.pallas_call(
        functools.partial(gradient_kernel, shape),
        in_specs=[anywhere] * 6 + [local] * 2,
        out_specs=[anywhere] * 2 + [local] * len(rings),
        out_shape=[
            jax.ShapeDtypeStruct((channels, 3 * channels), F32),
            jax.ShapeDtypeStruct((positions, groups) + tile, F32),
        ]
        + [pltpu.VMEM((ring, chunk_rows, COLS), F32) for ring in rings],
        scratch_shapes=buffers + semaphores + landing,
        compiler_params=pltpu.CompilerParams(
            collective_id=1,
            has_side_effects=True,
            vmem_limit_bytes=max(held + 5 * 1024 * 1024, 40 * 1024 * 1024),
        ),
        cost_estimate=pl.CostEstimate(
            flops=4 * tokens * channels * 3 * channels,
            bytes_accessed=8 * channels * 3 * channels,
            transcendentals=0,
        ),
    )(normed, dproj, w_master, x_packed, stats, direct, gain, gate_sums)


def place_kernel(shape, w_ref, hidden_ref, grad_ref, *refs):
    plans, timing, rings, chunk_rows = shape
    accs, refs = refs[: len(rings)], refs[len(rings) :]
    last_ref, w_out, grad_out, hidden_out, *refs = refs
    stream = timing.sums_stream
    totals_ref = accs[stream].at[timing.chunks[stream] % rings[stream]]
    sums, final = refs[:6], refs[6]
    w_ring, grad_ring, hidden_ring, kept_sem, *ring_sems = refs[7:]
    groups = sums[0].shape[0] // 2
    half = ROWS // 2
    row_blocks = w_ref.shape[0] // chunk_rows
    kept, first = kept_chunks(timing, rings, row_blocks)

    def kept_copy(order):
        index, number, slot = kept[order]
        rows = pl.ds(index % row_blocks * chunk_rows, chunk_rows)
        columns = pl.ds(index // row_blocks * COLS, COLS)
        return pltpu.make_async_copy(
            accs[number].at[slot], w_out.at[rows, columns], kept_sem.at[order]
        )

    class Through:

        def __init__(self, source, target, ring, sems, columns=None):
            self.source, self.target, self.ring, self.sems = source, target, ring, sems
            self.columns, self.slots, self.size = columns, ring.shape[0], ring.shape[1]
            self.pieces = source.shape[0] // self.size
            self.early = self.slots // 2

        def part(self, ref, piece):
            rows = pl.ds(pl.multiple_of(piece * self.size, self.size), self.size)
            return ref.at[rows] if self.columns is None else ref.at[rows, pl.ds(0, self.columns)]

        def read(self, piece):
            slot = lax.rem(piece, self.slots)
            return pltpu.make_async_copy(
                self.part(self.source, piece), self.ring.at[slot], self.sems.at[0, slot]
            )

        def write(self, piece):
            slot = lax.rem(piece, self.slots)
            return pltpu.make_async_copy(
                self.ring.at[slot], self.part(self.target, piece), self.sems.at[1, slot]
            )

        def begin(self):
            for piece in range(self.early):
                self.read(piece).start()

        def step(self, piece):
            self.read(piece).wait()
            self.write(piece).start()
            later = piece + self.early

            @pl.when(later < self.pieces)
            def _():
                @pl.when(later >= self.slots)
                def _():
                    self.write(later - self.slots).wait()

                self.read(later).start()

        def end(self):
            for piece in range(self.pieces - self.slots, self.pieces):
                self.write(piece).wait()

    w_way = Through(w_ref, w_out, w_ring, ring_sems[0], first * COLS)
    grad_way = Through(grad_ref, grad_out, grad_ring, ring_sems[1])
    hidden_way = Through(hidden_ref, hidden_out, hidden_ring, ring_sems[2])
    for way in (w_way, grad_way, hidden_way):
        way.begin()
    for order in range(len(kept)):
        kept_copy(order).start()

    for index, total in enumerate(sums):
        for group in range(groups):
            row = (index * groups + group) * ROWS
            tile = totals_ref[row : row + ROWS, :LANES]
            for part in range(2):
                line = jnp.sum(tile[part * half : (part + 1) * half], axis=0, keepdims=True)
                total[2 * group + part : 2 * group + part + 1, :] = line
    for group in range(last_ref.shape[0]):
        for part in range(2):
            columns = slice((2 * group + part) * LANES, (2 * group + part + 1) * LANES)
            final[:, columns] = last_ref[group, part * half : (part + 1) * half, :]

    every = w_way.pieces // grad_way.pieces

    @pl.loop(0, w_way.pieces)
    def _(piece):
        w_way.step(piece)

        @pl.when(lax.rem(piece, every) == 0)
        def _():
            grad_way.step(piece // every)
            hidden_way.step(piece // every)

    for way in (w_way, grad_way, hidden_way):
        way.end()
    for order in range(len(kept)):
        kept_copy(order).wait()


def kept_chunks(timing, rings, row_blocks):
    kept, lowest = [], 0
    for number, (chunks, ring) in enumerate(zip(timing.chunks, rings)):
        oldest = max(chunks + timing.sums(number) - ring, 0)
        for chunk in range(chunks):
            if chunk >= oldest:
                kept.append((timing.index(number, chunk), number, chunk % ring))
            else:
                lowest = max(lowest, timing.index(number, chunk) + 1)
    first = -(-lowest // row_blocks)
    return sorted(entry for entry in kept if entry[0] >= first * row_blocks), first


def place_results(shape, w_grad, out, input_grad, accs, final):
    plans, timing, rings, chunk_rows = shape
    channels = w_grad.shape[0]
    groups = channels // COLS
    kept, first = kept_chunks(timing, rings, channels // chunk_rows)
    local = pl.BlockSpec(memory_space=pltpu.VMEM)
    far = pl.BlockSpec(memory_space=pltpu.HBM)
    dma = pltpu.SemaphoreType.DMA
    small = [(2 * groups, LANES)] * 6 + [(ROWS // 2, final.shape[0] * COLS)]
    grad_piece = (input_grad.shape[0] // 16,) + input_grad.shape[1:]
    return pl.pallas_call(
        functools.partial(place_kernel, shape),
        in_specs=[far] * 3 + [local] * (len(accs) + 1),
        out_specs=[far] * 3 + [local] * len(small),
        out_shape=[
            jax.ShapeDtypeStruct(w_grad.shape, F32),
            jax.ShapeDtypeStruct(input_grad.shape, F32),
            jax.ShapeDtypeStruct(out.shape, BF16),
        ]
        + [jax.ShapeDtypeStruct(size, F32) for size in small],
        scratch_shapes=[
            pltpu.VMEM((16, channels // 64, first * COLS), F32),
            pltpu.VMEM((4,) + grad_piece, F32),
            pltpu.VMEM((4, out.shape[0] // 16, LANES), BF16),
            dma((len(kept),)),
            dma((2, 16)),
            dma((2, 4)),
            dma((2, 4)),
        ],
        compiler_params=pltpu.CompilerParams(vmem_limit_bytes=32 * 1024 * 1024),
        cost_estimate=pl.CostEstimate(
            flops=0, bytes_accessed=8 * w_grad.size + 8 * input_grad.size, transcendentals=0
        ),
    )(w_grad, out, input_grad, *accs, final)


def on_device(
    dp_count,
    sub_count,
    inputs,
    w_master,
    v_forget,
    v_reset,
    b_forget,
    b_reset,
    ln_gain,
    ln_shift,
    resets,
    cotangent,
):
    positions, seqs, channels = inputs.shape
    groups = channels // COLS

    def pack(tokens):
        split = tokens.reshape(positions, seqs, groups, 2, LANES)
        return split.transpose(0, 2, 3, 1, 4).reshape(positions * groups * ROWS, LANES)

    def unpack(packed):
        split = packed.reshape(positions, groups, 2, seqs, LANES)
        return split.transpose(0, 3, 1, 2, 4).reshape(positions, seqs, channels)

    def rows_of(vector):
        return vector.reshape(2 * groups, LANES)

    x_packed = pack(inputs)
    g_packed = pack(cotangent)
    gain, shift = rows_of(ln_gain), rows_of(ln_shift)

    proj, normed, stats, retain = project(
        x_packed, w_master, gain, shift, rows_of(b_forget), resets.T, positions
    )
    proj = proj.reshape(2, groups, positions, ROWS, LANES)
    out, direct, dproj, gate_sums, final = recur(
        proj,
        x_packed,
        g_packed,
        normed,
        w_master,
        retain,
        rows_of(v_forget),
        rows_of(v_reset),
        rows_of(b_reset),
        sub_count,
    )
    shape = gradient_plan(channels, dp_count, sub_count)
    w_grad, input_grad, *accs = gradients(
        shape, normed, dproj, w_master, x_packed, stats, direct, gain, gate_sums
    )
    w_grad, input_grad, out, *sums, final = place_results(
        shape, w_grad, out, input_grad, accs, final
    )
    sums = [total.reshape(channels) for total in sums]
    return (unpack(out), unpack(input_grad), w_grad, *sums, final)


def solution(mesh):
    placed = (
        P("sub", "dp", None),
        P(),
        P(),
        P(),
        P(),
        P(),
        P(),
        P(),
        P("sub", "dp"),
        P("sub", "dp", None),
    )
    return jax.shard_map(
        functools.partial(on_device, mesh.shape["dp"], mesh.shape["sub"]),
        mesh=mesh,
        in_specs=placed,
        out_specs=(
            P("sub", "dp", None),
            P("sub", "dp", None),
            P(),
            P(),
            P(),
            P(),
            P(),
            P(),
            P(),
            P("dp", "sub"),
        ),
        check_vma=False,
    )
```
